256 devices in a mesh: cell: 32 (over z, x), patch: 8 (over y, core).
Axes of the slice: x: 4, y: 4, z: 8, core: 2. Of those that a mesh axis runs over, the one named last changes fastest.
Arguments:
- right_side: float32 [1024, 3, 2112], P('cell', None, 'patch'), may hold values from -45 to 45
- analysis: float32 [2112, 1089], P('patch'), may hold values from -0.125 to 0.125
- spectral: float32 [1024, 1089], P('cell'), may hold values from 0.1 to 10
- near_kernel: float32 [2112, 2112], P(None, 'patch'), may hold values from -0.125 to 0.125
- near_send: int32 [32, 32, 8], P('cell'), may hold values from 0 to 31, as said below
- near_target: int32 [32, 32, 8], P('cell'), may hold values from -1 to 31, as said below
- near_strength: float32 [32, 32, 8], P('cell'), may hold values from 0.2 to 1
Outputs:
- solution: float32 [1024, 3, 2112], P('cell', None, 'patch')
- relative_residual: float32 [], replicated
The draws below stay inside these ranges and needn't reach their ends.
Inputs may be any that keep to these rules, and one draw needn't show every extreme that they name: `near_send`: each entry names one of the 32 cells of the sending group. Slot s of near_send[d, q] pairs with slot s of near_target[q, d]. Live slots come first. From group d to a group q at index distance at most one modulo 32 (d itself included) at most 8 slots are live, to any other group at most 2; both bounds are reached in every draw.
All inputs are finite; a program needn't handle non-finite values.
Results may differ from the reference program's by a relative error of at most 0.0003.
Values sent between devices are 32-bit elements; how exact they have to be, the bound alone decides.
No kernel may reach another device: no remote copies, remote signals or barrier semaphores. Data moves between devices by JAX's collectives and lax.ppermute only.
A program may use at most 128 MiB of HBM per device.

```python
import math
import jax
import jax.numpy as jnp
from jax import lax

PTS = 2112
COEF = 1089
CELL_DEV = 32
CAP = 8
FAR_CAP = 2
ITERS = 8
GROUPS = 32
NCELLS = 1024


def near_lists(key):
    keys = jax.random.split(jax.random.fold_in(key, 11), 6)
    sender = jnp.arange(GROUPS, dtype=jnp.int32)[:, None]
    receiver = jnp.arange(GROUPS, dtype=jnp.int32)[None, :]
    forward_gap = (receiver - sender) % GROUPS
    backward_gap = (sender - receiver) % GROUPS
    distance = jnp.minimum(forward_gap, backward_gap)
    close_count = jax.random.randint(keys[0], (GROUPS, GROUPS), CAP // 2, CAP + 1)
    far_count = jax.random.randint(keys[1], (GROUPS, GROUPS), 0, FAR_CAP + 1)
    counts = jnp.where(distance <= 1, close_count, far_count)
    full_pick = jax.random.randint(keys[2], (GROUPS, 1), 0, 3)
    full_peer = (sender + full_pick - 1 + GROUPS) % GROUPS
    counts = jnp.where(receiver == full_peer, CAP, counts)
    far_offset = jax.random.randint(keys[3], (GROUPS, 1), 2, GROUPS - 1)
    far_peer = (sender + far_offset) % GROUPS
    counts = jnp.where(receiver == far_peer, FAR_CAP, counts)
    send_cells = jax.random.randint(keys[4], (GROUPS, GROUPS, CAP), 0, CELL_DEV).astype(jnp.int32)
    raw_targets = jax.random.randint(keys[5], (GROUPS, GROUPS, CAP), 0, CELL_DEV)
    slot_ids = jnp.arange(CAP, dtype=jnp.int32)[None, None, :]
    live = slot_ids < counts[:, :, None]
    targets = jnp.where(live, raw_targets, -1).astype(jnp.int32)
    return (send_cells, jnp.transpose(targets, (1, 0, 2)))


def draw_near_send(key, part):
    return near_lists(key)[0]


def draw_near_target(key, part):
    return near_lists(key)[1]


def draw_right_side(key, part):
    keys = jax.random.split(jax.random.fold_in(key, 5), 2)
    base = jax.random.truncated_normal(keys[0], -4.0, 4.0, (NCELLS, 3, PTS), jnp.float32)
    rough = jnp.exp(jax.random.uniform(keys[1], (NCELLS, 1, 1), jnp.float32) * math.log(10.0))
    rising = (3.0 ** (jnp.arange(NCELLS, dtype=jnp.float32) / NCELLS)).reshape(NCELLS, 1, 1)
    return (0.3 * base * rough * rising).astype(jnp.float32)


def block_levels(rng, shape, shards, least, top_value):
    level = 1.0
    for axis_at, shards_of in shards:
        draws = jax.random.uniform(jax.random.fold_in(jax.random.fold_in(rng, 6), axis_at), (shards_of,), jnp.float32, least / len(shards), top_value / len(shards))
        level = level * jnp.repeat(jnp.exp(draws), shape[axis_at] // shards_of).reshape((-1,) + (1,) * (len(shape) - 1 - axis_at))
    return level


def gaussian(stream_key, dims, width, bound, shards=(), kind=jnp.bfloat16):
    factor_of = block_levels(stream_key, dims, shards, -0.22, 0.18) if shards else 1.0
    drawn = jax.random.normal(stream_key, dims, jnp.float32) * width * factor_of
    return jnp.minimum(jnp.maximum(drawn, -bound), bound).astype(kind)


def setup_inputs(seed: int = 0) -> dict:
    key_list = jax.random.split(jax.random.key(seed), 8)
    right_side = draw_right_side(jax.random.fold_in(key_list[7], 71), 0)
    analysis = gaussian(key_list[1], (PTS, COEF), PTS ** -0.5, 0.125, ((0, 8),), jnp.float32)
    spectral = jnp.clip(jnp.exp(math.log(10.0) - 4.6051702 * jax.random.uniform(key_list[2], (NCELLS, COEF), jnp.float32) ** block_levels(key_list[2], (NCELLS, COEF), ((0, 32),), -0.2, 0.2)), 0.1, 10.0)
    near_kernel = gaussian(key_list[3], (PTS, PTS), PTS ** -0.5, 0.125, ((1, 8),), jnp.float32)
    near_send = draw_near_send(jax.random.fold_in(key_list[7], 71), 0)
    near_target = draw_near_target(jax.random.fold_in(key_list[7], 71), 0)
    near_strength = jnp.clip(jnp.exp(math.log(1.0) - 1.609438 * jax.random.uniform(key_list[6], (GROUPS, GROUPS, CAP), jnp.float32) ** block_levels(key_list[6], (GROUPS, GROUPS, CAP), ((0, 32),), -0.2, 0.2)), 0.2, 1.0)
    return {"right_side": right_side, "analysis": analysis, "spectral": spectral, "near_kernel": near_kernel, "near_send": near_send, "near_target": near_target, "near_strength": near_strength}


HIGH_PRECISION = lax.Precision.HIGHEST

def small_solve(gram, right):
    lower = jnp.linalg.cholesky(gram)
    order = gram.shape[0]
    forward = []
    for row in range(order):
        value = right[row] - sum((lower[row, col] * forward[col] for col in range(row)))
        forward.append(value / lower[row, row])
    backward = [None] * order
    for row in reversed(range(order)):
        value = forward[row] - sum((lower[col, row] * backward[col] for col in range(row + 1, order)))
        backward[row] = value / lower[row, row]
    return jnp.stack(backward)

def apply_operator(vector, analysis, spectral, near_kernel, source_rows, target_cells, weights):

    def one_group(inputs):
        sources, targets, strengths = inputs
        blocks = vector[sources] * strengths[:, None, None]
        return jax.ops.segment_sum(blocks, jnp.maximum(targets, 0), num_segments=CELL_DEV)
    gathered = lax.map(one_group, (source_rows, target_cells, weights)).reshape(NCELLS, 3, PTS)
    coefficients = jnp.einsum('ncp,pk->nck', vector, analysis, precision=HIGH_PRECISION)
    self_term = jnp.einsum('nck,pk->ncp', coefficients * spectral[:, None, :], analysis, precision=HIGH_PRECISION)
    near_term = jnp.einsum('ncp,pq->ncq', gathered, near_kernel, precision=HIGH_PRECISION)
    return vector + self_term + near_term

def reference(right_side, analysis, spectral, near_kernel, near_send, near_target, near_strength):
    group_ids = jnp.arange(GROUPS, dtype=jnp.int32)
    source_rows = (group_ids[None, :, None] * CELL_DEV + jnp.transpose(near_send, (1, 0, 2))).astype(jnp.int32)
    source_rows = source_rows.reshape(GROUPS, GROUPS * CAP)
    target_cells = near_target.reshape(GROUPS, GROUPS * CAP)
    weights = jnp.where(near_target >= 0, near_strength, jnp.zeros_like(near_strength)).reshape(GROUPS, GROUPS * CAP)
    beta = jnp.sqrt(jnp.sum(right_side * right_side))
    basis = [right_side / beta]
    hessen = jnp.zeros((ITERS + 1, ITERS), jnp.float32)
    for column in range(ITERS):
        image = apply_operator(basis[column], analysis, spectral, near_kernel, source_rows, target_cells, weights)
        projected = jnp.stack([jnp.sum(earlier * image) for earlier in basis])
        image = image - sum((projected[member] * basis[member] for member in range(column + 1)))
        length = jnp.sqrt(jnp.sum(image * image))
        hessen = hessen.at[:column + 1, column].set(projected)
        hessen = hessen.at[column + 1, column].set(length)
        basis.append(image / length)
    gram = jnp.dot(hessen.T, hessen, precision=HIGH_PRECISION)
    coeffs = small_solve(gram, beta * hessen[0])
    solution = sum((coeffs[member] * basis[member] for member in range(ITERS)))
    target_vec = jnp.zeros((ITERS + 1,), jnp.float32).at[0].set(beta)
    misfit = target_vec - jnp.dot(hessen, coeffs, precision=HIGH_PRECISION)
    relative_residual = jnp.sqrt(jnp.sum(misfit * misfit)) / beta
    return (solution, relative_residual)
```

```python
import jax
import jax.numpy as jnp
from jax import lax
from jax.experimental import pallas as pl
from jax.experimental.pallas import tpu as pltpu
from jax.sharding import Mesh
from jax.sharding import PartitionSpec as P

CAP = 8
FAR_CAP = 2
CELL = ("cell_0", "cell_1")
PATCH = ("patch_0", "patch_1")
BLOCKS = (2, 3, 3)
NODES = (1.2, -1.2, 0.0, 0.6, -0.6)
FIRST_SHIFT = 1.0
FIRST_SCALE = 4.0
PRESCALE = 2.0**-16
ROWS_SENT = 8
KERNEL_VMEM = 52
F32 = jnp.float32
BF16 = jnp.bfloat16


def halves(x):
    high = x.astype(BF16)
    return high, (x - high.astype(F32)).astype(BF16)


def exact_halves(x):
    high = lax.reduce_precision(x, 8, 7)
    return high.astype(BF16), (x - high).astype(BF16)


def thirds(x):
    high = x.astype(BF16)
    rest = x - high.astype(F32)
    middle = rest.astype(BF16)
    return high, middle, (rest - middle.astype(F32)).astype(BF16)


def mul(a, b, dims=(((1,), (0,)), ((), ()))):
    return lax.dot_general(a, b, dims, preferred_element_type=F32)


def pair(x):
    return jnp.concatenate(halves(x), axis=1)


def mul_pair(high, low, both):
    rows = both.shape[1] // 2
    wide = mul(high[...], both)
    return wide[:, :rows] + wide[:, rows:] + mul(low[...], both[:, :rows])


def mul3(a, b, dims=(((1,), (0,)), ((), ()))):
    return mul(a[0], b[0], dims) + (mul(a[0], b[1], dims) + mul(a[1], b[0], dims))


class Staged:
    def __init__(self, ref, copy):
        self.ref, self.copy = ref, copy

    def __getitem__(self, at):
        if self.copy is not None:
            self.copy.wait()
            self.copy = None
        return self.ref[at]

    @property
    def shape(self):
        return self.ref.shape


def call(body, outs, *args, near=(), near_outs=(), flops=10**8, scratch=(), vmem=KERNEL_VMEM):
    flat = outs if isinstance(outs, tuple) else (outs,)
    n, m = len(args), len(flat)
    far = [k for k in range(n) if k not in near]
    far_outs = [k for k in range(m) if k not in near_outs]

    def wrapped(*refs):
        ins, results, rest = list(refs[:n]), list(refs[n : n + m]), refs[n + m :]
        stage, rest = rest[: len(far)], rest[len(far) :]
        stage_outs, rest = rest[: len(far_outs)], rest[len(far_outs) :]
        sems, own = rest[0], rest[1:]
        for at, k in enumerate(far):
            copy = pltpu.make_async_copy(ins[k], stage[at], sems.at[at])
            copy.start()
            ins[k] = Staged(stage[at], copy)
        views = list(results)
        for at, k in enumerate(far_outs):
            views[k] = stage_outs[at]

        def send(k):
            at = far_outs.index(k)
            copy = pltpu.make_async_copy(stage_outs[at], results[k], sems.at[len(far) + at])
            copy.start()
            sent[k] = copy

        sent = {}
        body(ins, views, own, send)
        for staged in ins:
            if isinstance(staged, Staged) and staged.copy is not None:
                staged.copy.wait()
        for k in far_outs:
            if k not in sent:
                send(k)
        for copy in sent.values():
            copy.wait()

    def place(k, close):
        return pl.BlockSpec(memory_space=pltpu.VMEM if k in close else pl.ANY)

    moved = sum(a.size * a.dtype.itemsize for a in args)
    result = pl.pallas_call(
        wrapped,
        out_shape=flat,
        in_specs=[place(k, near) for k in range(n)],
        out_specs=tuple(place(k, near_outs) for k in range(m)),
        scratch_shapes=[pltpu.VMEM(args[k].shape, args[k].dtype) for k in far]
        + [pltpu.VMEM(flat[k].shape, flat[k].dtype) for k in far_outs]
        + [pltpu.SemaphoreType.DMA((len(far) + len(far_outs) + 1,))]
        + list(scratch),
        compiler_params=pltpu.CompilerParams(vmem_limit_bytes=vmem * 1024 * 1024),
        cost_estimate=pl.CostEstimate(flops=flops, bytes_accessed=moved, transcendentals=0),
    )(*args)
    return result if isinstance(outs, tuple) else result[0]


def shape(*lengths):
    return jax.ShapeDtypeStruct(lengths, F32)


def gram_pairs(block):
    start = sum(BLOCKS[:block])
    end = start + BLOCKS[block]
    return [(i, j) for i in range(start, end + 1) for j in range(i + 1)]


class Small:
    def __init__(self, sums):
        self.t = {}
        self.shifts = []
        self.scales = []
        self.combine = []
        self.mean = FIRST_SHIFT
        self.spread = None
        self.scale = FIRST_SCALE
        gram = {}
        made = 0
        for block, steps in enumerate(BLOCKS):
            for step in range(steps):
                shift = self.mean
                if block and NODES[step]:
                    shift = shift + NODES[step] * self.spread
                self.shifts.append(shift)
                self.scales.append(self.scale)
                self.t[made, made] = shift
                self.t[made + 1, made] = self.scale
                made += 1
            if block >= len(sums):
                break
            values = sums[block]
            for at, (i, j) in enumerate(gram_pairs(block)):
                gram[i, j] = values[0:1, at : at + 1]
            self.r = self.factor(gram, made + 1)
            if block + 1 < len(BLOCKS):
                self.restart(gram, made)

    @staticmethod
    def factor(gram, order):
        r = {}
        for row in range(order):
            pivot = gram.get((row, row), 1.0) - sum(r[k, row] * r[k, row] for k in range(row) if (k, row) in r)
            r[row, row] = jnp.sqrt(pivot)
            inverse = 1.0 / r[row, row]
            for col in range(row + 1, order):
                if (col, row) not in gram:
                    continue
                value = gram[col, row] - sum(
                    r[k, row] * r[k, col] for k in range(row) if (k, row) in r and (k, col) in r
                )
                r[row, col] = value * inverse
        return r

    def restart(self, gram, m):
        r, t = self.r, self.t
        coefs = [None] * m
        for row in reversed(range(m)):
            value = r[row, m] - sum(
                r[row, k] * coefs[k] for k in range(row + 1, m) if (row, k) in r
            )
            coefs[row] = value / r[row, row]
        rho = r[m, m]
        gamma = t[m, m - 1]
        for row in range(m):
            t[row, m - 1] = t.get((row, m - 1), 0.0) + gamma * coefs[row]
        t[m, m - 1] = gamma * rho
        self.combine.append((coefs, 1.0 / rho))
        trace = sum(t[k, k] for k in range(m))
        square = sum(
            t[i, k] * t[k, i] for i in range(m) for k in range(m) if (i, k) in t and (k, i) in t
        )
        self.mean = trace * (1.0 / m)
        self.spread = jnp.sqrt(jnp.maximum(square * (1.0 / m) - self.mean * self.mean, 0.0))
        reach = jnp.abs(t[m, m - 1] / r[m - 1, m - 1])
        self.scale = jnp.maximum(jnp.maximum(reach, self.spread), 1e-3 * jnp.abs(self.mean))

    def least_squares(self):
        r, t = self.r, self.t
        n = sum(BLOCKS)
        h = {}
        for col in range(n):
            for row in range(col + 2):
                terms = [
                    r[row, k] * t[k, col]
                    for k in range(row, col + 2)
                    if (row, k) in r and (k, col) in t
                ]
                h[row, col] = sum(terms) if terms else jnp.zeros_like(r[0, 0])
        right = [r[0, 0]] + [jnp.zeros_like(r[0, 0])] * n
        for col in range(n):
            a, b = h[col, col], h[col + 1, col]
            inverse = lax.rsqrt(a * a + b * b)
            cos, sin = a * inverse, b * inverse
            for k in range(col, n):
                upper, lower = h[col, k], h[col + 1, k]
                h[col, k] = cos * upper + sin * lower
                h[col + 1, k] = cos * lower - sin * upper
            right[col], right[col + 1] = cos * right[col], -sin * right[col]
        y = [None] * n
        for row in reversed(range(n)):
            value = right[row] - sum(h[row, k] * y[k] for k in range(row + 1, n))
            y[row] = value / h[row, row]
        return y, jnp.abs(right[n]) / r[0, 0]


def in_lanes(values):
    lane = lax.broadcasted_iota(jnp.int32, (1, 128), 1)
    row = jnp.zeros((1, 128), F32)
    for at, value in enumerate(values):
        row = jnp.where(lane == at, value, row)
    return row


def plan_row(sums):
    block = len(sums)
    small = Small(sums)
    start = sum(BLOCKS[:block])
    steps = range(start, start + BLOCKS[block])
    coefs, inverse = small.combine[block - 1]
    row = in_lanes(
        [small.shifts[k] for k in steps] + [1.0 / small.scales[k] for k in steps] + coefs + [inverse]
    )
    return row, coefs, inverse


def restarted(sums, kept):
    m = len(kept) - 1
    count = len(sums)

    def body(ins, outs, own, send):
        row, coefs, inverse = plan_row([ref[...] for ref in ins[:count]])
        outs[2][...] = row
        send(2)
        vectors = ins[count:]
        total = vectors[m][...]
        for k in range(m):
            total -= coefs[k] * vectors[k][...]
        total = total * inverse
        outs[0][...] = total
        send(0)
        pack(total, outs[1])

    outs = (shape(*kept[0].shape), packed_shape(kept[0].shape[0]), shape(1, 128))
    return call(body, outs, *sums, *kept, near_outs=(1,))


def final_of(sums, kept):
    n, count = len(kept), len(sums)

    def body(ins, outs, own, send):
        y, residual = Small([ref[...] for ref in ins[:count]]).least_squares()
        vectors = ins[count:]
        total = y[0] * (1.0 / PRESCALE) * vectors[0][...]
        for k in range(1, n):
            total += y[k] * (1.0 / PRESCALE) * vectors[k][...]
        outs[0][...] = total
        outs[1][...] = in_lanes([residual])

    return call(body, (shape(*kept[0].shape), shape(1, 128)), *sums, *kept)


def local_sums(block, kept):
    pairs = gram_pairs(block)

    def body(ins, outs, own, send):
        vectors = [ref[...] for ref in ins]
        rows = [jnp.sum(vectors[i] * vectors[j], axis=0, keepdims=True) for i, j in pairs]
        rows += [jnp.zeros_like(rows[0])] * (-len(rows) % 8)
        sums = jnp.sum(jnp.concatenate(rows, axis=0), axis=1, keepdims=True)
        row = lax.broadcasted_iota(jnp.int32, (len(rows), 128), 0)
        lane = lax.broadcasted_iota(jnp.int32, (len(rows), 128), 1)
        outs[0][...] = jnp.sum(jnp.where(row == lane, sums, 0.0), axis=0, keepdims=True)

    return call(body, shape(1, 128), *kept, near_outs=(0,))


def total_over(x, axes):
    copies = jnp.broadcast_to(x, (lax.axis_size(axes), *x.shape))
    return lax.all_to_all(copies, axes, 0, 0, tiled=True).sum(0)


def from_ahead(x, axis, by):
    n = lax.axis_size(axis)
    return lax.ppermute(x, axis, [(i, (i - by) % n) for i in range(n)])


def spread(x):
    near = [x] + [from_ahead(x, "patch_0", by) for by in (1, 3, 2)]
    return near + [from_ahead(x, "patch_1", 1) for x in near]


def patches_by_distance():
    me0, me1 = lax.axis_index("patch_0"), lax.axis_index("patch_1")
    n0, n1 = lax.axis_size("patch_0"), lax.axis_size("patch_1")
    return [
        lax.rem(me0 + by, n0) * n1 + lax.rem(me1 + across, n1) for across in range(2) for by in (0, 1, 3, 2)
    ]


def tail_of(length):
    return length // 4 // 8 * 8


def pack(x, out):
    length, lanes = x.shape
    tail = tail_of(length)
    keep = length - tail
    free = 128 - lanes
    out[:, lanes:] = jnp.zeros((keep, free), F32)
    out[:, :lanes] = x[:keep]
    for at in range(lanes // free):
        out[at * tail : (at + 1) * tail, lanes:] = x[keep:, at * free : (at + 1) * free]


def unpack(packed, whole, offset, lanes):
    keep, wide = packed.shape
    free = wide - lanes
    length = keep + tail_of(whole.shape[0] // 8)
    tail = length - keep
    whole[pl.ds(pl.multiple_of(offset, 8), keep), :] = packed[:, :lanes]
    for at in range(lanes // free):
        whole[pl.ds(pl.multiple_of(offset + keep, 8), tail), at * free : (at + 1) * free] = packed[
            at * tail : (at + 1) * tail, lanes:
        ]


def packed_shape(length):
    return shape(length - tail_of(length), 128)


def packed_of(x):
    def body(ins, outs, own, send):
        pack(ins[0][...], outs[0])

    return call(body, packed_shape(x.shape[0]), x, near_outs=(0,))


def near_kernel_of(blocks, high, low, points, rows, select_far, select_near):
    n = len(blocks)

    def body(ins, outs, own, send):
        whole = own[0]
        wh, wl, far_ref, near_ref = ins[n:]
        for packed, at in zip(ins[:n], patches_by_distance(), strict=True):
            unpack(packed, whole, at * points, rows)
        both = pair(whole[...])
        outs[4][...] = both
        send(4)
        w = mul_pair(wh, wl, both)[:points]
        outs[3][...] = w
        send(3)
        pieces = thirds(w)

        def chosen(g):
            return sum(mul(g, piece, (((1,), (1,)), ((), ()))) for piece in pieces)

        outs[0][...] = chosen(far_ref[...])
        send(0)
        close = chosen(near_ref[...])
        half = close.shape[0] // 2
        outs[1][...] = close[:half]
        outs[2][...] = close[half:]

    half = select_near.shape[0] // 2
    outs = (
        shape(select_far.shape[0], points),
        shape(half, points),
        shape(half, points),
        shape(points, rows),
        jax.ShapeDtypeStruct((n * points, 2 * rows), BF16),
    )
    args = (*blocks, high, low, select_far, select_near)
    scratch = [pltpu.VMEM((n * points, rows), F32)]
    return call(body, outs, *args, near=range(n), flops=10**9, scratch=scratch)


def columns_of(parts):
    count, rows, length = parts.shape
    top = -(-rows // 32) * 16

    def body(ins, outs, own, send):
        for k in range(count):
            for at, cut in ((0, slice(0, top)), (1, slice(top, rows))):
                high, low = halves(ins[0][...][k][cut])
                outs[2 * at][:, k * length : (k + 1) * length] = high
                outs[2 * at + 1][:, k * length : (k + 1) * length] = low

    outs = tuple(
        jax.ShapeDtypeStruct((length_of, count * length), BF16) for length_of in (top, top, rows - top, rows - top)
    )
    return call(body, outs, parts)


def coefficients_of(both, columns, spectral):
    def body(ins, outs, own, send):
        both_ref, sp = ins[:2]
        both = both_ref[...]
        done = 0
        for at in range(2, len(ins), 2):
            part = mul_pair(ins[at], ins[at + 1], both)
            cut = slice(done, done + part.shape[0])
            outs[0][cut] = part * sp[cut]
            done += part.shape[0]

    return call(body, shape(*spectral.shape), both, spectral, *columns, flops=2 * 10**9)


def partial_coefficients(vector, forth):
    def body(ins, outs, own, send):
        outs[0][...] = mul3(halves(ins[1][...]), halves(ins[0][...]))

    return call(body, shape(forth.shape[0], vector.shape[1]), vector, forth)


def self_part(mine, other, high, low, w, placed_own):
    half, rows = mine.shape
    points = w.shape[0]

    def body(ins, outs, own, send):
        mine_ref, other_ref, bh, bl, w_ref, own_ref = ins
        whole = own[0]
        me1 = lax.axis_index("patch_1")
        whole[pl.ds(pl.multiple_of(me1 * half, 8), half), :] = mine_ref[...]
        whole[pl.ds(pl.multiple_of((1 - me1) * half, 8), half), :] = other_ref[...]
        total = mul_pair(bh, bl, pair(whole[...]))[:points]
        outs[0][...] = total + mul3(halves(w_ref[...]), halves(own_ref[...]))

    args = (mine, other, high, low, w, placed_own)
    scratch = [pltpu.VMEM((2 * half, rows), F32)]
    return call(body, shape(*w.shape), *args, near=(0, 1), flops=5 * 10**8, scratch=scratch)


def advanced(plan, block, step, vector, local, received, targets):
    def body(ins, outs, own, send):
        plan_ref, v_ref, local_ref = ins[:3]
        count = len(received)
        total = local_ref[...]
        for k in reversed(range(count)):
            total += mul3(
                halves(ins[3 + k][...]), halves(ins[3 + count + k][...]), (((0,), (0,)), ((), ()))
            )
        if block:
            plan = plan_ref[...]
            shift = plan[0:1, step : step + 1]
            inverse = plan[0:1, BLOCKS[block] + step : BLOCKS[block] + step + 1]
        else:
            shift, inverse = FIRST_SHIFT, 1.0 / FIRST_SCALE
        result = (total + (1.0 - shift) * v_ref[...]) * inverse
        outs[0][...] = result
        send(0)
        pack(result, outs[1])

    outs = (shape(*vector.shape), packed_shape(vector.shape[0]))
    return call(body, outs, plan, vector, local, *received, *targets, near_outs=(1,))


def per_device(right_side, analysis, spectral, near_kernel, near_send, near_target, near_strength):
    cells, comps, points = right_side.shape
    rows = cells * comps
    groups = lax.axis_size(CELL)
    me = lax.axis_index(CELL)
    after, before = (me + 1) % groups, (me + groups - 1) % groups

    lane = jnp.arange(rows, dtype=jnp.int32)

    def by_row(table):
        return jnp.repeat(table, comps, axis=-1)

    def of_group(table, group):
        return lax.dynamic_index_in_dim(table, group, 0, keepdims=False)

    comp = jnp.tile(jnp.arange(comps, dtype=jnp.int32), CAP)
    sends = by_row(near_send[0]) * comps + comp
    live = near_target[0] >= 0
    places = by_row(near_target[0]) * comps + comp
    strengths = by_row(jnp.where(live, near_strength[0], 0.0))
    gap = (jnp.arange(groups, dtype=jnp.int32) - me) % groups
    distant = (gap > 1) & (gap < groups - 1)

    def selected(at):
        return (at.reshape(-1, 1) == lane).astype(F32)

    def placed(at, by):
        return jnp.where(at.reshape(-1, 1) == lane, by.reshape(-1, 1), 0.0)

    used = FAR_CAP * comps
    pad = ((0, 0), (0, ROWS_SENT - used))
    select_far = selected(jnp.pad(sends[:, :used], pad, constant_values=-1)).astype(BF16)
    place_far = placed(
        jnp.pad(places[:, :used], pad, constant_values=-1),
        jnp.pad(jnp.where(distant[:, None], strengths[:, :used], 0.0), pad),
    )
    select_near = selected(jnp.concatenate([of_group(sends, after), of_group(sends, before)])).astype(BF16)
    place_next, place_prev = (placed(of_group(places, g), of_group(strengths, g)) for g in (after, before))
    own = lax.dot_general(
        selected(of_group(sends, me)),
        placed(of_group(places, me), of_group(strengths, me)),
        (((0,), (0,)), ((), ())),
        precision=lax.Precision.HIGHEST,
    )

    half = -(-analysis.shape[1] // 2)
    half = -(-half // 16) * 16
    back = jnp.pad(analysis, ((0, -points % 16), (0, 2 * half - analysis.shape[1])))
    forth = back.T[:, :points]
    back = exact_halves(back)
    me1 = lax.axis_index("patch_1")
    first = me1 == 0
    mine = jnp.where(first, forth[:half], forth[half:])
    theirs = from_ahead(jnp.where(first, forth[half:], forth[:half]), "patch_1", 1)
    columns = jnp.concatenate([jnp.where(first, mine, theirs), jnp.where(first, theirs, mine)], 1)
    columns = columns_of(lax.all_gather(columns, "patch_0"))
    near = near_kernel.T
    near = exact_halves(jnp.pad(near, ((0, -near.shape[0] % 16), (0, 0))))
    scale = jnp.pad(spectral, ((0, 0), (0, 2 * half - spectral.shape[1]))).T
    scale = lax.dynamic_slice_in_dim(scale, me1 * half, half, 0)
    scale = jnp.repeat(scale, comps, axis=1)

    def first_coefficients(vector):
        parts = partial_coefficients(vector, forth)
        mine = jnp.where(first, parts[:half], parts[half:])
        theirs = jnp.where(first, parts[half:], parts[:half])
        chip = mine + from_ahead(theirs, "patch_1", 1)
        total = chip + sum(from_ahead(chip, "patch_0", by) for by in (1, 3, 2))
        return total * scale

    def apply(vector, packed, plan, at, step, known=None):
        blocks = spread(packed)
        far, to_next, to_prev, w, both = near_kernel_of(
            blocks, *near, points, rows, select_far, select_near
        )
        from_prev = from_ahead(to_next, CELL, -1)
        from_next = from_ahead(to_prev, CELL, 1)
        received = lax.all_to_all(far.reshape(groups, ROWS_SENT, points), CELL, 0, 0, tiled=True)
        coefs = coefficients_of(both, columns, scale) if known is None else known
        coefs, from_prev, from_next = lax.optimization_barrier((coefs, from_prev, from_next))
        local = self_part(coefs, from_ahead(coefs, "patch_1", 1), *back, w, own)
        return advanced(
            plan,
            at,
            step,
            vector,
            local,
            (received.reshape(-1, points), from_next, from_prev),
            (place_far, place_next, place_prev),
        )

    kept = [right_side.reshape(rows, points).T * PRESCALE]
    packed = packed_of(kept[0])
    sums = []
    plan = jnp.zeros((1, 128), F32)
    for at, steps in enumerate(BLOCKS):
        if at:
            kept[-1], packed, plan = restarted(sums, kept)
        for step in range(steps):
            known = first_coefficients(kept[0]) if at == step == 0 else None
            vector, packed = apply(kept[-1], packed, plan, at, step, known)
            kept.append(vector)
        sums.append(total_over(total_over(local_sums(at, kept), CELL), PATCH))
    result, residual = final_of(sums, kept[:-1])
    return result.T.reshape(cells, comps, points), residual[0, 0]


def solution(mesh):
    torus = Mesh(mesh.devices.reshape(8, 4, 4, 2), ("cell_0", "cell_1", "patch_0", "patch_1"))
    return jax.shard_map(
        per_device,
        mesh=torus,
        in_specs=(
            P(CELL, None, PATCH),
            P(PATCH, None),
            P(CELL, None),
            P(None, PATCH),
            P(CELL, None, None),
            P(CELL, None, None),
            P(CELL, None, None),
        ),
        out_specs=(P(CELL, None, PATCH), P()),
        check_vma=False,
    )
```

```python
import jax
import jax.numpy as jnp
from jax import lax
from jax.experimental import pallas as pl
from jax.experimental.pallas import tpu as pltpu
from jax.sharding import Mesh
from jax.sharding import PartitionSpec as P

CAP = 8
FAR_CAP = 2
CELL = ("cell_0", "cell_1")
PATCH = ("patch_0", "patch_1")
BLOCKS = (2, 3, 3)
NODES = (1.2, -1.2, 0.0, 0.6, -0.6)
FIRST_SHIFT = 1.0
FIRST_SCALE = 4.0
PRESCALE = 2.0**-16
ROWS_SENT = 8
KERNEL_VMEM = 52
F32 = jnp.float32
BF16 = jnp.bfloat16


def halves(x):
    high = x.astype(BF16)
    return high, (x - high.astype(F32)).astype(BF16)


def exact_halves(x):
    high = lax.reduce_precision(x, 8, 7)
    return high.astype(BF16), (x - high).astype(BF16)


def thirds(x):
    high = x.astype(BF16)
    rest = x - high.astype(F32)
    middle = rest.astype(BF16)
    return high, middle, (rest - middle.astype(F32)).astype(BF16)


def mul(a, b, dims=(((1,), (0,)), ((), ()))):
    return lax.dot_general(a, b, dims, preferred_element_type=F32)


def pair(x):
    return jnp.concatenate(halves(x), axis=1)


def mul_pair(high, low, both):
    rows = both.shape[1] // 2
    wide = mul(high[...], both)
    return wide[:, :rows] + wide[:, rows:] + mul(low[...], both[:, :rows])


def mul3(a, b, dims=(((1,), (0,)), ((), ()))):
    return mul(a[0], b[0], dims) + (mul(a[0], b[1], dims) + mul(a[1], b[0], dims))


class Staged:
    def __init__(self, ref, copy):
        self.ref, self.copy = ref, copy

    def __getitem__(self, at):
        if self.copy is not None:
            self.copy.wait()
            self.copy = None
        return self.ref[at]

    @property
    def shape(self):
        return self.ref.shape


def call(body, outs, *args, near=(), near_outs=(), flops=10**8, scratch=(), vmem=KERNEL_VMEM):
    flat = outs if isinstance(outs, tuple) else (outs,)
    n, m = len(args), len(flat)
    far = [k for k in range(n) if k not in near]
    far_outs = [k for k in range(m) if k not in near_outs]

    def wrapped(*refs):
        ins, results, rest = list(refs[:n]), list(refs[n : n + m]), refs[n + m :]
        stage, rest = rest[: len(far)], rest[len(far) :]
        stage_outs, rest = rest[: len(far_outs)], rest[len(far_outs) :]
        sems, own = rest[0], rest[1:]
        for at, k in enumerate(far):
            copy = pltpu.make_async_copy(ins[k], stage[at], sems.at[at])
            copy.start()
            ins[k] = Staged(stage[at], copy)
        views = list(results)
        for at, k in enumerate(far_outs):
            views[k] = stage_outs[at]

        def send(k):
            at = far_outs.index(k)
            copy = pltpu.make_async_copy(stage_outs[at], results[k], sems.at[len(far) + at])
            copy.start()
            sent[k] = copy

        sent = {}
        body(ins, views, own, send)
        for staged in ins:
            if isinstance(staged, Staged) and staged.copy is not None:
                staged.copy.wait()
        for k in far_outs:
            if k not in sent:
                send(k)
        for copy in sent.values():
            copy.wait()

    def place(k, close):
        return pl.BlockSpec(memory_space=pltpu.VMEM if k in close else pl.ANY)

    moved = sum(a.size * a.dtype.itemsize for a in args) if flops > 1 else 1
    result = pl.pallas_call(
        wrapped,
        out_shape=flat,
        in_specs=[place(k, near) for k in range(n)],
        out_specs=tuple(place(k, near_outs) for k in range(m)),
        scratch_shapes=[pltpu.VMEM(args[k].shape, args[k].dtype) for k in far]
        + [pltpu.VMEM(flat[k].shape, flat[k].dtype) for k in far_outs]
        + [pltpu.SemaphoreType.DMA((len(far) + len(far_outs) + 1,))]
        + list(scratch),
        compiler_params=pltpu.CompilerParams(vmem_limit_bytes=vmem * 1024 * 1024),
        cost_estimate=pl.CostEstimate(flops=flops, bytes_accessed=moved, transcendentals=0),
    )(*args)
    return result if isinstance(outs, tuple) else result[0]


def shape(*lengths):
    return jax.ShapeDtypeStruct(lengths, F32)


def gram_pairs(block):
    start = sum(BLOCKS[:block])
    end = start + BLOCKS[block]
    return [(i, j) for i in range(start, end + 1) for j in range(i + 1)]


class Small:
    def __init__(self, sums):
        self.t = {}
        self.shifts = []
        self.scales = []
        self.combine = []
        self.mean = FIRST_SHIFT
        self.spread = None
        self.scale = FIRST_SCALE
        gram = {}
        made = 0
        for block, steps in enumerate(BLOCKS):
            for step in range(steps):
                shift = self.mean
                if block and NODES[step]:
                    shift = shift + NODES[step] * self.spread
                self.shifts.append(shift)
                self.scales.append(self.scale)
                self.t[made, made] = shift
                self.t[made + 1, made] = self.scale
                made += 1
            if block >= len(sums):
                break
            values = sums[block]
            for at, (i, j) in enumerate(gram_pairs(block)):
                gram[i, j] = values[0:1, at : at + 1]
            self.r = self.factor(gram, made + 1)
            if block + 1 < len(BLOCKS):
                self.restart(gram, made)

    @staticmethod
    def factor(gram, order):
        r = {}
        for row in range(order):
            pivot = gram.get((row, row), 1.0) - sum(r[k, row] * r[k, row] for k in range(row) if (k, row) in r)
            r[row, row] = jnp.sqrt(pivot)
            inverse = 1.0 / r[row, row]
            for col in range(row + 1, order):
                if (col, row) not in gram:
                    continue
                value = gram[col, row] - sum(
                    r[k, row] * r[k, col] for k in range(row) if (k, row) in r and (k, col) in r
                )
                r[row, col] = value * inverse
        return r

    def restart(self, gram, m):
        r, t = self.r, self.t
        coefs = [None] * m
        for row in reversed(range(m)):
            value = r[row, m] - sum(
                r[row, k] * coefs[k] for k in range(row + 1, m) if (row, k) in r
            )
            coefs[row] = value / r[row, row]
        rho = r[m, m]
        gamma = t[m, m - 1]
        for row in range(m):
            t[row, m - 1] = t.get((row, m - 1), 0.0) + gamma * coefs[row]
        t[m, m - 1] = gamma * rho
        self.combine.append((coefs, 1.0 / rho))
        trace = sum(t[k, k] for k in range(m))
        square = sum(
            t[i, k] * t[k, i] for i in range(m) for k in range(m) if (i, k) in t and (k, i) in t
        )
        self.mean = trace * (1.0 / m)
        self.spread = jnp.sqrt(jnp.maximum(square * (1.0 / m) - self.mean * self.mean, 0.0))
        reach = jnp.abs(t[m, m - 1] / r[m - 1, m - 1])
        self.scale = jnp.maximum(jnp.maximum(reach, self.spread), 1e-3 * jnp.abs(self.mean))

    def least_squares(self):
        r, t = self.r, self.t
        n = sum(BLOCKS)
        h = {}
        for col in range(n):
            for row in range(col + 2):
                terms = [
                    r[row, k] * t[k, col]
                    for k in range(row, col + 2)
                    if (row, k) in r and (k, col) in t
                ]
                h[row, col] = sum(terms) if terms else jnp.zeros_like(r[0, 0])
        right = [r[0, 0]] + [jnp.zeros_like(r[0, 0])] * n
        for col in range(n):
            a, b = h[col, col], h[col + 1, col]
            inverse = lax.rsqrt(a * a + b * b)
            cos, sin = a * inverse, b * inverse
            for k in range(col, n):
                upper, lower = h[col, k], h[col + 1, k]
                h[col, k] = cos * upper + sin * lower
                h[col + 1, k] = cos * lower - sin * upper
            right[col], right[col + 1] = cos * right[col], -sin * right[col]
        y = [None] * n
        for row in reversed(range(n)):
            value = right[row] - sum(h[row, k] * y[k] for k in range(row + 1, n))
            y[row] = value / h[row, row]
        return y, jnp.abs(right[n]) / r[0, 0]


def in_lanes(values):
    lane = lax.broadcasted_iota(jnp.int32, (1, 128), 1)
    row = jnp.zeros((1, 128), F32)
    for at, value in enumerate(values):
        row = jnp.where(lane == at, value, row)
    return row


def plan_row(sums):
    block = len(sums)
    small = Small(sums)
    start = sum(BLOCKS[:block])
    steps = range(start, start + BLOCKS[block])
    coefs, inverse = small.combine[block - 1]
    row = in_lanes(
        [small.shifts[k] for k in steps] + [1.0 / small.scales[k] for k in steps] + coefs + [inverse]
    )
    return row, coefs, inverse


def restarted(sums, kept):
    m = len(kept) - 1
    count = len(sums)

    def body(ins, outs, own, send):
        row, coefs, inverse = plan_row([ref[...] for ref in ins[:count]])
        outs[2][...] = row
        send(2)
        vectors = ins[count:]
        total = vectors[m][...]
        for k in range(m):
            total -= coefs[k] * vectors[k][...]
        total = total * inverse
        outs[0][...] = total
        send(0)
        pack(total, outs[1])

    outs = (shape(*kept[0].shape), packed_shape(kept[0].shape[0]), shape(1, 128))
    return call(body, outs, *sums, *kept, near_outs=(1,))


def final_of(sums, kept):
    n, count = len(kept), len(sums)

    def body(ins, outs, own, send):
        y, residual = Small([ref[...] for ref in ins[:count]]).least_squares()
        vectors = ins[count:]
        total = y[0] * (1.0 / PRESCALE) * vectors[0][...]
        for k in range(1, n):
            total += y[k] * (1.0 / PRESCALE) * vectors[k][...]
        outs[0][...] = total
        outs[1][...] = in_lanes([residual])

    return call(body, (shape(*kept[0].shape), shape(1, 128)), *sums, *kept)


def local_sums(block, kept):
    pairs = gram_pairs(block)

    def body(ins, outs, own, send):
        vectors = [ref[...] for ref in ins]
        rows = [jnp.sum(vectors[i] * vectors[j], axis=0, keepdims=True) for i, j in pairs]
        rows += [jnp.zeros_like(rows[0])] * (-len(rows) % 8)
        sums = jnp.sum(jnp.concatenate(rows, axis=0), axis=1, keepdims=True)
        row = lax.broadcasted_iota(jnp.int32, (len(rows), 128), 0)
        lane = lax.broadcasted_iota(jnp.int32, (len(rows), 128), 1)
        outs[0][...] = jnp.sum(jnp.where(row == lane, sums, 0.0), axis=0, keepdims=True)

    return call(body, shape(1, 128), *kept, near_outs=(0,))


def total_over(x, axes):
    copies = jnp.broadcast_to(x, (lax.axis_size(axes), *x.shape))
    return lax.all_to_all(copies, axes, 0, 0, tiled=True).sum(0)


def from_ahead(x, axis, by):
    n = lax.axis_size(axis)
    return lax.ppermute(x, axis, [(i, (i - by) % n) for i in range(n)])


def spread(x):
    near = [x] + [from_ahead(x, "patch_0", by) for by in (1, 3, 2)]
    return near + [from_ahead(x, "patch_1", 1) for x in near]


def patches_by_distance():
    me0, me1 = lax.axis_index("patch_0"), lax.axis_index("patch_1")
    n0, n1 = lax.axis_size("patch_0"), lax.axis_size("patch_1")
    return [
        lax.rem(me0 + by, n0) * n1 + lax.rem(me1 + across, n1) for across in range(2) for by in (0, 1, 3, 2)
    ]


def tail_of(length):
    return length // 4 // 8 * 8


def pack(x, out):
    length, lanes = x.shape
    tail = tail_of(length)
    keep = length - tail
    free = 128 - lanes
    out[:, lanes:] = jnp.zeros((keep, free), F32)
    out[:, :lanes] = x[:keep]
    for at in range(lanes // free):
        out[at * tail : (at + 1) * tail, lanes:] = x[keep:, at * free : (at + 1) * free]


def unpack(packed, whole, offset, lanes):
    keep, wide = packed.shape
    free = wide - lanes
    length = keep + tail_of(whole.shape[0] // 8)
    tail = length - keep
    whole[pl.ds(pl.multiple_of(offset, 8), keep), :] = packed[:, :lanes]
    for at in range(lanes // free):
        whole[pl.ds(pl.multiple_of(offset + keep, 8), tail), at * free : (at + 1) * free] = packed[
            at * tail : (at + 1) * tail, lanes:
        ]


def packed_shape(length):
    return shape(length - tail_of(length), 128)


def packed_of(x):
    def body(ins, outs, own, send):
        pack(ins[0][...], outs[0])

    return call(body, packed_shape(x.shape[0]), x, near_outs=(0,))


def near_kernel_of(blocks, high, low, points, rows, select_far, select_near):
    n = len(blocks)

    def body(ins, outs, own, send):
        whole = own[0]
        wh, wl, far_ref, near_ref = ins[n:]
        for packed, at in zip(ins[:n], patches_by_distance(), strict=True):
            unpack(packed, whole, at * points, rows)
        both = pair(whole[...])
        outs[4][...] = both
        send(4)
        w = mul_pair(wh, wl, both)[:points]
        outs[3][...] = w
        send(3)
        pieces = thirds(w)

        def chosen(g):
            return sum(mul(g, piece, (((1,), (1,)), ((), ()))) for piece in pieces)

        outs[0][...] = chosen(far_ref[...])
        send(0)
        close = chosen(near_ref[...])
        half = close.shape[0] // 2
        outs[1][...] = close[:half]
        outs[2][...] = close[half:]

    half = select_near.shape[0] // 2
    outs = (
        shape(select_far.shape[0], points),
        shape(half, points),
        shape(half, points),
        shape(points, rows),
        jax.ShapeDtypeStruct((n * points, 2 * rows), BF16),
    )
    args = (*blocks, high, low, select_far, select_near)
    scratch = [pltpu.VMEM((n * points, rows), F32)]
    return call(body, outs, *args, near=range(n), flops=10**9, scratch=scratch)


def columns_of(parts):
    count, length, rows = parts.shape
    top = -(-rows // 32) * 16

    def body(ins, outs, own, send):
        for k in range(count):
            part = ins[0][...][k].T
            for at, cut in ((0, slice(0, top)), (1, slice(top, rows))):
                high, low = halves(part[cut])
                outs[2 * at][:, k * length : (k + 1) * length] = high
                outs[2 * at + 1][:, k * length : (k + 1) * length] = low

    outs = tuple(
        jax.ShapeDtypeStruct((length_of, count * length), BF16) for length_of in (top, top, rows - top, rows - top)
    )
    return call(body, outs, parts)


def coefficients_of(both, columns, spectral):
    def body(ins, outs, own, send):
        both_ref, sp = ins[:2]
        both = both_ref[...]
        done = 0
        for at in range(2, len(ins), 2):
            part = mul_pair(ins[at], ins[at + 1], both)
            cut = slice(done, done + part.shape[0])
            outs[0][cut] = part * sp[cut]
            done += part.shape[0]

    return call(body, shape(*spectral.shape), both, spectral, *columns, flops=10**10)


def partial_coefficients(vector, forth):
    def body(ins, outs, own, send):
        outs[0][...] = mul3(halves(ins[1][...]), halves(ins[0][...]))

    return call(body, shape(forth.shape[0], vector.shape[1]), vector, forth)


def self_part(mine, other, high, low, w, placed_own):
    half, rows = mine.shape
    points = w.shape[0]

    def body(ins, outs, own, send):
        mine_ref, other_ref, bh, bl, w_ref, own_ref = ins
        whole = own[0]
        me1 = lax.axis_index("patch_1")
        whole[pl.ds(pl.multiple_of(me1 * half, 8), half), :] = mine_ref[...]
        whole[pl.ds(pl.multiple_of((1 - me1) * half, 8), half), :] = other_ref[...]
        total = mul_pair(bh, bl, pair(whole[...]))[:points]
        outs[0][...] = total + mul3(halves(w_ref[...]), halves(own_ref[...]))

    args = (mine, other, high, low, w, placed_own)
    scratch = [pltpu.VMEM((2 * half, rows), F32)]
    return call(body, shape(*w.shape), *args, near=(0, 1), flops=5 * 10**8, scratch=scratch)


def advanced(plan, block, step, vector, local, received, targets):
    def body(ins, outs, own, send):
        plan_ref, v_ref, local_ref = ins[:3]
        count = len(received)
        total = local_ref[...]
        for k in reversed(range(count)):
            total += mul3(
                halves(ins[3 + k][...]), halves(ins[3 + count + k][...]), (((0,), (0,)), ((), ()))
            )
        if block:
            plan = plan_ref[...]
            shift = plan[0:1, step : step + 1]
            inverse = plan[0:1, BLOCKS[block] + step : BLOCKS[block] + step + 1]
        else:
            shift, inverse = FIRST_SHIFT, 1.0 / FIRST_SCALE
        result = (total + (1.0 - shift) * v_ref[...]) * inverse
        outs[0][...] = result
        send(0)
        pack(result, outs[1])

    outs = (shape(*vector.shape), packed_shape(vector.shape[0]))
    return call(body, outs, plan, vector, local, *received, *targets, near_outs=(1,))


def per_device(right_side, analysis, spectral, near_kernel, near_send, near_target, near_strength):
    cells, comps, points = right_side.shape
    rows = cells * comps
    groups = lax.axis_size(CELL)
    me = lax.axis_index(CELL)
    after, before = (me + 1) % groups, (me + groups - 1) % groups

    lane = jnp.arange(rows, dtype=jnp.int32)

    def by_row(table):
        return jnp.repeat(table, comps, axis=-1)

    def of_group(table, group):
        return lax.dynamic_index_in_dim(table, group, 0, keepdims=False)

    comp = jnp.tile(jnp.arange(comps, dtype=jnp.int32), CAP)
    sends = by_row(near_send[0]) * comps + comp
    live = near_target[0] >= 0
    places = by_row(near_target[0]) * comps + comp
    strengths = by_row(jnp.where(live, near_strength[0], 0.0))
    gap = (jnp.arange(groups, dtype=jnp.int32) - me) % groups
    distant = (gap > 1) & (gap < groups - 1)

    def selected(at):
        return (at.reshape(-1, 1) == lane).astype(F32)

    def placed(at, by):
        return jnp.where(at.reshape(-1, 1) == lane, by.reshape(-1, 1), 0.0)

    used = FAR_CAP * comps
    pad = ((0, 0), (0, ROWS_SENT - used))
    select_far = selected(jnp.pad(sends[:, :used], pad, constant_values=-1)).astype(BF16)
    place_far = placed(
        jnp.pad(places[:, :used], pad, constant_values=-1),
        jnp.pad(jnp.where(distant[:, None], strengths[:, :used], 0.0), pad),
    )
    select_near = selected(jnp.concatenate([of_group(sends, after), of_group(sends, before)])).astype(BF16)
    place_next, place_prev = (placed(of_group(places, g), of_group(strengths, g)) for g in (after, before))
    own = lax.dot_general(
        selected(of_group(sends, me)),
        placed(of_group(places, me), of_group(strengths, me)),
        (((0,), (0,)), ((), ())),
        precision=lax.Precision.HIGHEST,
    )

    half = -(-analysis.shape[1] // 2)
    half = -(-half // 16) * 16
    back = jnp.pad(analysis, ((0, -points % 16), (0, 2 * half - analysis.shape[1])))
    forth = back.T[:, :points]
    back = exact_halves(back)
    me1 = lax.axis_index("patch_1")
    first = me1 == 0
    wide = jnp.pad(analysis, ((0, 0), (0, 2 * half - analysis.shape[1])))
    mine = jnp.where(first, wide[:, :half], wide[:, half:])
    theirs = from_ahead(jnp.where(first, wide[:, half:], wide[:, :half]), "patch_1", 1)
    columns = jnp.concatenate([jnp.where(first, mine, theirs), jnp.where(first, theirs, mine)])
    columns = columns_of(lax.all_gather(columns, "patch_0"))
    near = near_kernel.T
    near = exact_halves(jnp.pad(near, ((0, -near.shape[0] % 16), (0, 0))))
    scale = jnp.pad(spectral, ((0, 0), (0, 2 * half - spectral.shape[1]))).T
    scale = lax.dynamic_slice_in_dim(scale, me1 * half, half, 0)
    scale = jnp.repeat(scale, comps, axis=1)

    def first_coefficients(vector):
        parts = partial_coefficients(vector, forth)
        mine = jnp.where(first, parts[:half], parts[half:])
        theirs = jnp.where(first, parts[half:], parts[:half])
        chip = mine + from_ahead(theirs, "patch_1", 1)
        total = chip + sum(from_ahead(chip, "patch_0", by) for by in (1, 3, 2))
        return total * scale

    def apply(vector, packed, plan, at, step, known=None):
        blocks = spread(packed)
        far, to_next, to_prev, w, both = near_kernel_of(
            blocks, *near, points, rows, select_far, select_near
        )
        from_prev = from_ahead(to_next, CELL, -1)
        from_next = from_ahead(to_prev, CELL, 1)
        received = lax.all_to_all(far.reshape(groups, ROWS_SENT, points), CELL, 0, 0, tiled=True)
        both, from_prev, from_next = lax.optimization_barrier((both, from_prev, from_next))
        coefs = coefficients_of(both, columns, scale) if known is None else known
        local = self_part(coefs, from_ahead(coefs, "patch_1", 1), *back, w, own)
        return advanced(
            plan,
            at,
            step,
            vector,
            local,
            (received.reshape(-1, points), from_next, from_prev),
            (place_far, place_next, place_prev),
        )

    kept = [right_side.reshape(rows, points).T * PRESCALE]
    packed = packed_of(kept[0])
    sums = []
    plan = jnp.zeros((1, 128), F32)
    for at, steps in enumerate(BLOCKS):
        if at:
            kept[-1], packed, plan = restarted(sums, kept)
        for step in range(steps):
            known = first_coefficients(kept[0]) if at == step == 0 else None
            vector, packed = apply(kept[-1], packed, plan, at, step, known)
            kept.append(vector)
        sums.append(total_over(total_over(local_sums(at, kept), CELL), PATCH))
    result, residual = final_of(sums, kept[:-1])
    return result.T.reshape(cells, comps, points), residual[0, 0]


def solution(mesh):
    torus = Mesh(mesh.devices.reshape(8, 4, 4, 2), ("cell_0", "cell_1", "patch_0", "patch_1"))
    return jax.shard_map(
        per_device,
        mesh=torus,
        in_specs=(
            P(CELL, None, PATCH),
            P(PATCH, None),
            P(CELL, None),
            P(None, PATCH),
            P(CELL, None, None),
            P(CELL, None, None),
            P(CELL, None, None),
        ),
        out_specs=(P(CELL, None, PATCH), P()),
        check_vma=False,
    )
```

```python
import jax
import jax.numpy as jnp
from jax import lax
from jax.experimental import pallas as pl
from jax.experimental.pallas import tpu as pltpu
from jax.sharding import Mesh
from jax.sharding import PartitionSpec as P

CAP = 8
FAR_CAP = 2
CELL = ("cell_0", "cell_1")
PATCH = ("patch_0", "patch_1")
BLOCKS = (2, 3, 3)
NODES = (1.2, -1.2, 0.0, 0.6, -0.6)
FIRST_SHIFT = 1.0
FIRST_SCALE = 4.0
PRESCALE = 2.0**-16
FAR_ROWS = FAR_CAP * 3
ROWS_SENT = 8
KERNEL_VMEM = 52
F32 = jnp.float32
BF16 = jnp.bfloat16


def halves(x):
    high = x.astype(BF16)
    return high, (x - high.astype(F32)).astype(BF16)


def exact_halves(x):
    high = lax.reduce_precision(x, 8, 7)
    return high.astype(BF16), (x - high).astype(BF16)


def thirds(x):
    high = x.astype(BF16)
    rest = x - high.astype(F32)
    middle = rest.astype(BF16)
    return high, middle, (rest - middle.astype(F32)).astype(BF16)


def mul(a, b, dims=(((1,), (0,)), ((), ()))):
    return lax.dot_general(a, b, dims, preferred_element_type=F32)


def pair(x):
    return jnp.concatenate(halves(x), axis=1)


def mul_pair(high, low, both):
    rows = both.shape[1] // 2
    wide = mul(high[...], both)
    return wide[:, :rows] + wide[:, rows:] + mul(low[...], both[:, :rows])


def mul3(a, b, dims=(((1,), (0,)), ((), ()))):
    return mul(a[0], b[0], dims) + (mul(a[0], b[1], dims) + mul(a[1], b[0], dims))


class Staged:
    def __init__(self, ref, copy):
        self.ref, self.copy = ref, copy

    def __getitem__(self, at):
        if self.copy is not None:
            self.copy.wait()
            self.copy = None
        return self.ref[at]

    @property
    def shape(self):
        return self.ref.shape


def call(body, outs, *args, near=(), near_outs=(), flops=10**8, scratch=(), vmem=KERNEL_VMEM):
    flat = outs if isinstance(outs, tuple) else (outs,)
    n, m = len(args), len(flat)
    far = [k for k in range(n) if k not in near]
    far_outs = [k for k in range(m) if k not in near_outs]

    def wrapped(*refs):
        ins, results, rest = list(refs[:n]), list(refs[n : n + m]), refs[n + m :]
        stage, rest = rest[: len(far)], rest[len(far) :]
        stage_outs, rest = rest[: len(far_outs)], rest[len(far_outs) :]
        sems, own = rest[0], rest[1:]
        for at, k in enumerate(far):
            copy = pltpu.make_async_copy(ins[k], stage[at], sems.at[at])
            copy.start()
            ins[k] = Staged(stage[at], copy)
        views = list(results)
        for at, k in enumerate(far_outs):
            views[k] = stage_outs[at]

        def send(k):
            at = far_outs.index(k)
            copy = pltpu.make_async_copy(stage_outs[at], results[k], sems.at[len(far) + at])
            copy.start()
            sent[k] = copy

        sent = {}
        body(ins, views, own, send)
        for staged in ins:
            if isinstance(staged, Staged) and staged.copy is not None:
                staged.copy.wait()
        for k in far_outs:
            if k not in sent:
                send(k)
        for copy in sent.values():
            copy.wait()

    def place(k, close):
        return pl.BlockSpec(memory_space=pltpu.VMEM if k in close else pl.ANY)

    moved = sum(a.size * a.dtype.itemsize for a in args) if flops > 1 else 1
    result = pl.pallas_call(
        wrapped,
        out_shape=flat,
        in_specs=[place(k, near) for k in range(n)],
        out_specs=tuple(place(k, near_outs) for k in range(m)),
        scratch_shapes=[pltpu.VMEM(args[k].shape, args[k].dtype) for k in far]
        + [pltpu.VMEM(flat[k].shape, flat[k].dtype) for k in far_outs]
        + [pltpu.SemaphoreType.DMA((len(far) + len(far_outs) + 1,))]
        + list(scratch),
        compiler_params=pltpu.CompilerParams(vmem_limit_bytes=vmem * 1024 * 1024),
        cost_estimate=pl.CostEstimate(flops=flops, bytes_accessed=moved, transcendentals=0),
    )(*args)
    return result if isinstance(outs, tuple) else result[0]


def shape(*lengths):
    return jax.ShapeDtypeStruct(lengths, F32)


def gram_pairs(block):
    start = sum(BLOCKS[:block])
    end = start + BLOCKS[block]
    return [(i, j) for i in range(start, end + 1) for j in range(i + 1)]


class Small:
    def __init__(self, sums):
        self.t = {}
        self.shifts = []
        self.scales = []
        self.combine = []
        self.mean = FIRST_SHIFT
        self.spread = None
        self.scale = FIRST_SCALE
        gram = {}
        made = 0
        for block, steps in enumerate(BLOCKS):
            for step in range(steps):
                shift = self.mean
                if block and NODES[step]:
                    shift = shift + NODES[step] * self.spread
                self.shifts.append(shift)
                self.scales.append(self.scale)
                self.t[made, made] = shift
                self.t[made + 1, made] = self.scale
                made += 1
            if block >= len(sums):
                break
            values = sums[block]
            for at, (i, j) in enumerate(gram_pairs(block)):
                gram[i, j] = values[0:1, at : at + 1]
            self.r = self.factor(gram, made + 1)
            if block + 1 < len(BLOCKS):
                self.restart(gram, made)

    @staticmethod
    def factor(gram, order):
        r = {}
        for row in range(order):
            pivot = gram.get((row, row), 1.0) - sum(r[k, row] * r[k, row] for k in range(row) if (k, row) in r)
            r[row, row] = jnp.sqrt(pivot)
            inverse = 1.0 / r[row, row]
            for col in range(row + 1, order):
                if (col, row) not in gram:
                    continue
                value = gram[col, row] - sum(
                    r[k, row] * r[k, col] for k in range(row) if (k, row) in r and (k, col) in r
                )
                r[row, col] = value * inverse
        return r

    def restart(self, gram, m):
        r, t = self.r, self.t
        coefs = [None] * m
        for row in reversed(range(m)):
            value = r[row, m] - sum(
                r[row, k] * coefs[k] for k in range(row + 1, m) if (row, k) in r
            )
            coefs[row] = value / r[row, row]
        rho = r[m, m]
        gamma = t[m, m - 1]
        for row in range(m):
            t[row, m - 1] = t.get((row, m - 1), 0.0) + gamma * coefs[row]
        t[m, m - 1] = gamma * rho
        self.combine.append((coefs, 1.0 / rho))
        trace = sum(t[k, k] for k in range(m))
        square = sum(
            t[i, k] * t[k, i] for i in range(m) for k in range(m) if (i, k) in t and (k, i) in t
        )
        self.mean = trace * (1.0 / m)
        self.spread = jnp.sqrt(jnp.maximum(square * (1.0 / m) - self.mean * self.mean, 0.0))
        reach = jnp.abs(t[m, m - 1] / r[m - 1, m - 1])
        self.scale = jnp.maximum(jnp.maximum(reach, self.spread), 1e-3 * jnp.abs(self.mean))

    def least_squares(self):
        r, t = self.r, self.t
        n = sum(BLOCKS)
        h = {}
        for col in range(n):
            for row in range(col + 2):
                terms = [
                    r[row, k] * t[k, col]
                    for k in range(row, col + 2)
                    if (row, k) in r and (k, col) in t
                ]
                h[row, col] = sum(terms) if terms else jnp.zeros_like(r[0, 0])
        right = [r[0, 0]] + [jnp.zeros_like(r[0, 0])] * n
        for col in range(n):
            a, b = h[col, col], h[col + 1, col]
            inverse = lax.rsqrt(a * a + b * b)
            cos, sin = a * inverse, b * inverse
            for k in range(col, n):
                upper, lower = h[col, k], h[col + 1, k]
                h[col, k] = cos * upper + sin * lower
                h[col + 1, k] = cos * lower - sin * upper
            right[col], right[col + 1] = cos * right[col], -sin * right[col]
        y = [None] * n
        for row in reversed(range(n)):
            value = right[row] - sum(h[row, k] * y[k] for k in range(row + 1, n))
            y[row] = value / h[row, row]
        return y, jnp.abs(right[n]) / r[0, 0]


def in_lanes(values):
    lane = lax.broadcasted_iota(jnp.int32, (1, 128), 1)
    row = jnp.zeros((1, 128), F32)
    for at, value in enumerate(values):
        row = jnp.where(lane == at, value, row)
    return row


def plan_row(sums):
    block = len(sums)
    small = Small(sums)
    start = sum(BLOCKS[:block])
    steps = range(start, start + BLOCKS[block])
    coefs, inverse = small.combine[block - 1]
    row = in_lanes(
        [small.shifts[k] for k in steps] + [1.0 / small.scales[k] for k in steps] + coefs + [inverse]
    )
    return row, coefs, inverse


def restarted(sums, kept):
    m = len(kept) - 1
    count = len(sums)

    def body(ins, outs, own, send):
        row, coefs, inverse = plan_row([ref[...] for ref in ins[:count]])
        outs[2][...] = row
        send(2)
        vectors = ins[count:]
        total = vectors[m][...]
        for k in range(m):
            total -= coefs[k] * vectors[k][...]
        total = total * inverse
        outs[0][...] = total
        send(0)
        pack(total, outs[1])

    outs = (shape(*kept[0].shape), packed_shape(kept[0].shape[0]), shape(1, 128))
    return call(body, outs, *sums, *kept, near_outs=(1,))


def final_of(sums, kept):
    n, count = len(kept), len(sums)

    def body(ins, outs, own, send):
        y, residual = Small([ref[...] for ref in ins[:count]]).least_squares()
        vectors = ins[count:]
        total = y[0] * (1.0 / PRESCALE) * vectors[0][...]
        for k in range(1, n):
            total += y[k] * (1.0 / PRESCALE) * vectors[k][...]
        outs[0][...] = total
        outs[1][...] = in_lanes([residual])

    return call(body, (shape(*kept[0].shape), shape(1, 128)), *sums, *kept)


def local_sums(block, kept):
    pairs = gram_pairs(block)

    def body(ins, outs, own, send):
        vectors = [ref[...] for ref in ins]
        rows = [jnp.sum(vectors[i] * vectors[j], axis=0, keepdims=True) for i, j in pairs]
        rows += [jnp.zeros_like(rows[0])] * (-len(rows) % 8)
        sums = jnp.sum(jnp.concatenate(rows, axis=0), axis=1, keepdims=True)
        row = lax.broadcasted_iota(jnp.int32, (len(rows), 128), 0)
        lane = lax.broadcasted_iota(jnp.int32, (len(rows), 128), 1)
        outs[0][...] = jnp.sum(jnp.where(row == lane, sums, 0.0), axis=0, keepdims=True)

    return call(body, shape(1, 128), *kept, near_outs=(0,))


def total_over(x, axes):
    copies = jnp.broadcast_to(x, (lax.axis_size(axes), *x.shape))
    return lax.all_to_all(copies, axes, 0, 0, tiled=True).sum(0)


def from_ahead(x, axis, by):
    n = lax.axis_size(axis)
    return lax.ppermute(x, axis, [(i, (i - by) % n) for i in range(n)])


def spread(x):
    near = [x] + [from_ahead(x, "patch_0", by) for by in (1, 3, 2)]
    return near + [from_ahead(x, "patch_1", 1) for x in near]


def patches_by_distance():
    me0, me1 = lax.axis_index("patch_0"), lax.axis_index("patch_1")
    n0, n1 = lax.axis_size("patch_0"), lax.axis_size("patch_1")
    return [
        lax.rem(me0 + by, n0) * n1 + lax.rem(me1 + across, n1) for across in range(2) for by in (0, 1, 3, 2)
    ]


def tail_of(length):
    return length // 4 // 8 * 8


def pack(x, out):
    length, lanes = x.shape
    tail = tail_of(length)
    keep = length - tail
    free = 128 - lanes
    out[:, lanes:] = jnp.zeros((keep, free), F32)
    out[:, :lanes] = x[:keep]
    for at in range(lanes // free):
        out[at * tail : (at + 1) * tail, lanes:] = x[keep:, at * free : (at + 1) * free]


def unpack(packed, whole, offset, lanes):
    keep, wide = packed.shape
    free = wide - lanes
    length = keep + tail_of(whole.shape[0] // 8)
    tail = length - keep
    whole[pl.ds(pl.multiple_of(offset, 8), keep), :] = packed[:, :lanes]
    for at in range(lanes // free):
        whole[pl.ds(pl.multiple_of(offset + keep, 8), tail), at * free : (at + 1) * free] = packed[
            at * tail : (at + 1) * tail, lanes:
        ]


def packed_shape(length):
    return shape(length - tail_of(length), 128)


def packed_of(x):
    def body(ins, outs, own, send):
        pack(ins[0][...], outs[0])

    return call(body, packed_shape(x.shape[0]), x, near_outs=(0,))


def tail_places(rows):
    row = lax.broadcasted_iota(jnp.int32, (rows, 128), 0) % ROWS_SENT
    return row, lax.broadcasted_iota(jnp.int32, (rows, 128), 1)


def folded(x, used):
    rows, points = x.shape
    wide = points // 128 * 128
    rest = points - wide
    tail = jnp.concatenate([x[:, wide:], jnp.zeros((rows, 128 - rest), F32)], axis=1)
    row, lane = tail_places(rows)
    extra = jnp.zeros((rows, 128), F32)
    for slot in range(used):
        moved = pltpu.roll(tail, used - slot, 0)
        if slot:
            moved = pltpu.roll(moved, rest * slot, 1)
        here = (row == used) & (lane >= rest * slot) & (lane < rest * (slot + 1))
        extra = jnp.where(here, moved, extra)
    return jnp.concatenate([x[:, :128] + extra, x[:, 128:wide]], axis=1)


def unfolded(x, points, used):
    rows, wide = x.shape
    rest = points - wide
    row, lane = tail_places(rows)
    tail = jnp.zeros((rows, 128), F32)
    for slot in range(used):
        moved = pltpu.roll(x[:, :128], rows - (used - slot), 0)
        if slot:
            moved = pltpu.roll(moved, 128 - rest * slot, 1)
        tail = jnp.where((row == slot) & (lane < rest), moved, tail)
    return jnp.concatenate([x, tail[:, :rest]], axis=1)


def near_kernel_of(blocks, high, low, points, rows, select_far, select_near):
    n = len(blocks)

    def body(ins, outs, own, send):
        whole = own[0]
        wh, wl, far_ref, near_ref = ins[n:]
        for packed, at in zip(ins[:n], patches_by_distance(), strict=True):
            unpack(packed, whole, at * points, rows)
        both = pair(whole[...])
        outs[4][...] = both
        send(4)
        w = mul_pair(wh, wl, both)[:points]
        outs[3][...] = w
        send(3)
        pieces = thirds(w)

        def chosen(g):
            return sum(mul(g, piece, (((1,), (1,)), ((), ()))) for piece in pieces)

        outs[0][...] = folded(chosen(far_ref[...]), FAR_ROWS)
        send(0)
        close = chosen(near_ref[...])
        half = close.shape[0] // 2
        outs[1][...] = close[:half]
        outs[2][...] = close[half:]

    half = select_near.shape[0] // 2
    outs = (
        shape(select_far.shape[0], points // 128 * 128),
        shape(half, points),
        shape(half, points),
        shape(points, rows),
        jax.ShapeDtypeStruct((n * points, 2 * rows), BF16),
    )
    args = (*blocks, high, low, select_far, select_near)
    scratch = [pltpu.VMEM((n * points, rows), F32)]
    return call(body, outs, *args, near=range(n), flops=10**9, scratch=scratch)


def columns_of(parts):
    count, length, rows = parts.shape
    top = -(-rows // 32) * 16

    def body(ins, outs, own, send):
        for k in range(count):
            part = ins[0][...][k].T
            for at, cut in ((0, slice(0, top)), (1, slice(top, rows))):
                high, low = halves(part[cut])
                outs[2 * at][:, k * length : (k + 1) * length] = high
                outs[2 * at + 1][:, k * length : (k + 1) * length] = low

    outs = tuple(
        jax.ShapeDtypeStruct((length_of, count * length), BF16) for length_of in (top, top, rows - top, rows - top)
    )
    return call(body, outs, parts)


def coefficients_of(both, columns, spectral):
    def body(ins, outs, own, send):
        both_ref, sp = ins[:2]
        both = both_ref[...]
        done = 0
        for at in range(2, len(ins), 2):
            part = mul_pair(ins[at], ins[at + 1], both)
            cut = slice(done, done + part.shape[0])
            outs[0][cut] = part * sp[cut]
            done += part.shape[0]

    return call(body, shape(*spectral.shape), both, spectral, *columns, flops=10**10)


def partial_coefficients(vector, forth):
    def body(ins, outs, own, send):
        outs[0][...] = mul3(halves(ins[1][...]), halves(ins[0][...]))

    return call(body, shape(forth.shape[0], vector.shape[1]), vector, forth)


def self_part(mine, other, high, low, w, placed_own):
    half, rows = mine.shape
    points = w.shape[0]

    def body(ins, outs, own, send):
        mine_ref, other_ref, bh, bl, w_ref, own_ref = ins
        whole = own[0]
        me1 = lax.axis_index("patch_1")
        whole[pl.ds(pl.multiple_of(me1 * half, 8), half), :] = mine_ref[...]
        whole[pl.ds(pl.multiple_of((1 - me1) * half, 8), half), :] = other_ref[...]
        total = mul_pair(bh, bl, pair(whole[...]))[:points]
        outs[0][...] = total + mul3(halves(w_ref[...]), halves(own_ref[...]))

    args = (mine, other, high, low, w, placed_own)
    scratch = [pltpu.VMEM((2 * half, rows), F32)]
    return call(body, shape(*w.shape), *args, near=(0, 1), flops=5 * 10**8, scratch=scratch)


def advanced(plan, block, step, vector, local, received, targets):
    def body(ins, outs, own, send):
        plan_ref, v_ref, local_ref = ins[:3]
        count = len(received)
        total = local_ref[...]
        for k in reversed(range(count)):
            rows_in = ins[3 + k][...]
            if rows_in.shape[1] < total.shape[0]:
                rows_in = unfolded(rows_in, total.shape[0], FAR_ROWS)
            total += mul3(
                halves(rows_in), halves(ins[3 + count + k][...]), (((0,), (0,)), ((), ()))
            )
        if block:
            plan = plan_ref[...]
            shift = plan[0:1, step : step + 1]
            inverse = plan[0:1, BLOCKS[block] + step : BLOCKS[block] + step + 1]
        else:
            shift, inverse = FIRST_SHIFT, 1.0 / FIRST_SCALE
        result = (total + (1.0 - shift) * v_ref[...]) * inverse
        outs[0][...] = result
        send(0)
        pack(result, outs[1])

    outs = (shape(*vector.shape), packed_shape(vector.shape[0]))
    return call(body, outs, plan, vector, local, *received, *targets, near_outs=(1,))


def per_device(right_side, analysis, spectral, near_kernel, near_send, near_target, near_strength):
    cells, comps, points = right_side.shape
    rows = cells * comps
    groups = lax.axis_size(CELL)
    me = lax.axis_index(CELL)
    after, before = (me + 1) % groups, (me + groups - 1) % groups

    lane = jnp.arange(rows, dtype=jnp.int32)

    def by_row(table):
        return jnp.repeat(table, comps, axis=-1)

    def of_group(table, group):
        return lax.dynamic_index_in_dim(table, group, 0, keepdims=False)

    comp = jnp.tile(jnp.arange(comps, dtype=jnp.int32), CAP)
    sends = by_row(near_send[0]) * comps + comp
    live = near_target[0] >= 0
    places = by_row(near_target[0]) * comps + comp
    strengths = by_row(jnp.where(live, near_strength[0], 0.0))
    gap = (jnp.arange(groups, dtype=jnp.int32) - me) % groups
    distant = (gap > 1) & (gap < groups - 1)

    def selected(at):
        return (at.reshape(-1, 1) == lane).astype(F32)

    def placed(at, by):
        return jnp.where(at.reshape(-1, 1) == lane, by.reshape(-1, 1), 0.0)

    used = FAR_CAP * comps
    pad = ((0, 0), (0, ROWS_SENT - used))
    select_far = selected(jnp.pad(sends[:, :used], pad, constant_values=-1)).astype(BF16)
    place_far = placed(
        jnp.pad(places[:, :used], pad, constant_values=-1),
        jnp.pad(jnp.where(distant[:, None], strengths[:, :used], 0.0), pad),
    )
    select_near = selected(jnp.concatenate([of_group(sends, after), of_group(sends, before)])).astype(BF16)
    place_next, place_prev = (placed(of_group(places, g), of_group(strengths, g)) for g in (after, before))
    own = lax.dot_general(
        selected(of_group(sends, me)),
        placed(of_group(places, me), of_group(strengths, me)),
        (((0,), (0,)), ((), ())),
        precision=lax.Precision.HIGHEST,
    )

    half = -(-analysis.shape[1] // 2)
    half = -(-half // 16) * 16
    back = jnp.pad(analysis, ((0, -points % 16), (0, 2 * half - analysis.shape[1])))
    forth = back.T[:, :points]
    back = exact_halves(back)
    me1 = lax.axis_index("patch_1")
    first = me1 == 0
    wide = jnp.pad(analysis, ((0, 0), (0, 2 * half - analysis.shape[1])))
    mine = jnp.where(first, wide[:, :half], wide[:, half:])
    theirs = from_ahead(jnp.where(first, wide[:, half:], wide[:, :half]), "patch_1", 1)
    columns = jnp.concatenate([jnp.where(first, mine, theirs), jnp.where(first, theirs, mine)])
    columns = columns_of(lax.all_gather(columns, "patch_0"))
    near = near_kernel.T
    near = exact_halves(jnp.pad(near, ((0, -near.shape[0] % 16), (0, 0))))
    scale = jnp.pad(spectral, ((0, 0), (0, 2 * half - spectral.shape[1]))).T
    scale = lax.dynamic_slice_in_dim(scale, me1 * half, half, 0)
    scale = jnp.repeat(scale, comps, axis=1)

    def first_coefficients(vector):
        parts = partial_coefficients(vector, forth)
        mine = jnp.where(first, parts[:half], parts[half:])
        theirs = jnp.where(first, parts[half:], parts[:half])
        chip = mine + from_ahead(theirs, "patch_1", 1)
        total = chip + sum(from_ahead(chip, "patch_0", by) for by in (1, 3, 2))
        return total * scale

    def apply(vector, packed, plan, at, step, known=None):
        blocks = spread(packed)
        far, to_next, to_prev, w, both = near_kernel_of(
            blocks, *near, points, rows, select_far, select_near
        )
        from_prev = from_ahead(to_next, CELL, -1)
        from_next = from_ahead(to_prev, CELL, 1)
        received = lax.all_to_all(far.reshape(groups, ROWS_SENT, far.shape[1]), CELL, 0, 0, tiled=True)
        both, from_prev, from_next = lax.optimization_barrier((both, from_prev, from_next))
        coefs = coefficients_of(both, columns, scale) if known is None else known
        local = self_part(coefs, from_ahead(coefs, "patch_1", 1), *back, w, own)
        return advanced(
            plan,
            at,
            step,
            vector,
            local,
            (received.reshape(-1, far.shape[1]), from_next, from_prev),
            (place_far, place_next, place_prev),
        )

    kept = [right_side.reshape(rows, points).T * PRESCALE]
    packed = packed_of(kept[0])
    sums = []
    plan = jnp.zeros((1, 128), F32)
    for at, steps in enumerate(BLOCKS):
        if at:
            kept[-1], packed, plan = restarted(sums, kept)
        for step in range(steps):
            known = first_coefficients(kept[0]) if at == step == 0 else None
            vector, packed = apply(kept[-1], packed, plan, at, step, known)
            kept.append(vector)
        sums.append(total_over(total_over(local_sums(at, kept), CELL), PATCH))
    result, residual = final_of(sums, kept[:-1])
    return result.T.reshape(cells, comps, points), residual[0, 0]


def solution(mesh):
    torus = Mesh(mesh.devices.reshape(8, 4, 4, 2), ("cell_0", "cell_1", "patch_0", "patch_1"))
    return jax.shard_map(
        per_device,
        mesh=torus,
        in_specs=(
            P(CELL, None, PATCH),
            P(PATCH, None),
            P(CELL, None),
            P(None, PATCH),
            P(CELL, None, None),
            P(CELL, None, None),
            P(CELL, None, None),
        ),
        out_specs=(P(CELL, None, PATCH), P()),
        check_vma=False,
    )
```
